256 devices in a mesh: dom: 128 (over z, y, x), grp: 2 (over core).
Axes of the slice: x: 4, y: 4, z: 8, core: 2. Of those that a mesh axis runs over, the one named last changes fastest.
Arguments:
- feats: bfloat16 [393216, 128], P(('dom', 'grp')), may hold values from -6 to 6
- local_adj: bfloat16 [393216, 1536], P(('dom', 'grp')), may hold values from 0 to 2, as said below
- bnd_adj: bfloat16 [256, 6, 1536, 256], P(('dom', 'grp')), may hold values from 0 to 2, as said below
- send_index: int32 [256, 6, 256], P(('dom', 'grp')), may hold values from 0 to 1535
- w_self: bfloat16 [128, 256], replicated, may hold values from -0.5 to 0.5
- w_neigh: bfloat16 [128, 256], replicated, may hold values from -4 to 4
- bias: float32 [256], replicated, may hold values from -3 to 3
- cotangent: bfloat16 [393216, 256], P(('dom', 'grp')), may hold values from -6 to 6
Outputs:
- output: bfloat16 [393216, 256], P(('dom', 'grp'))
- grad_feats: bfloat16 [393216, 128], P(('dom', 'grp'))
- grad_self: float32 [128, 256], replicated
- grad_neigh: float32 [128, 256], replicated
The draws below stay inside these ranges and needn't reach their ends.
Inputs may be any that keep to these rules, and one draw needn't show every extreme that they name: `local_adj`: edge weights are zero or between 0.5 and 2; most entries are zero. `bnd_adj`: edge weights are zero or between 0.5 and 2; most entries are zero.
All inputs are finite; a program needn't handle non-finite values.
Results may differ from the reference program's by a relative error of at most 0.0064.
Values may be sent and summed in bfloat16 or wider, within the bound.
No kernel may reach another device: no remote copies, remote signals or barrier semaphores. Data moves between devices by JAX's collectives and lax.ppermute only.
A program may use at most 128 MiB of HBM per device.

```python
import math
import jax
import jax.numpy as jnp
import numpy as np
from jax import lax

F = 128
H = 256
N_LOC = 1536
BND = 256
ROUNDS = 6
PARTS_SIZE = 256
NODES = 393216
N_DOM = 128
N_GRP = 2


def tiled_weights(key, lead, row_tiles, row_edge, col_tiles, col_edge, active_share, inner_density, diagonal):
    first, second, third = jax.random.split(key, 3)
    active = jax.random.uniform(first, lead + (row_tiles, col_tiles)) < active_share
    if diagonal:
        active = active | jnp.eye(row_tiles, col_tiles, dtype=bool)
    keep = jax.random.uniform(second, lead + (row_tiles, row_edge, col_tiles, col_edge)) < inner_density
    keep = keep & active[..., :, None, :, None]
    weight = jax.random.uniform(third, keep.shape, minval=0.5, maxval=2.0)
    return jnp.where(keep, weight, 0.0).astype(jnp.float32)


def draw_local_adj(key, part):
    key = jax.random.fold_in(key, 11)
    edge = min(128, N_LOC // 4)
    count = N_LOC // edge
    blocks = tiled_weights(key, (NODES // N_LOC,), count, edge, count, edge, 0.25, 0.04, True)
    return blocks.reshape(NODES, N_LOC).astype(jnp.bfloat16)


def draw_bnd_adj(key, part):
    key = jax.random.fold_in(key, 23)
    row_edge = min(128, N_LOC // 4)
    col_edge = min(128, BND // 2)
    blocks = tiled_weights(key, (PARTS_SIZE, ROUNDS), N_LOC // row_edge, row_edge, BND // col_edge, col_edge, 0.25, 0.02, False)
    return blocks.reshape(PARTS_SIZE, ROUNDS, N_LOC, BND).astype(jnp.bfloat16)


def touch_ends(entries, rng, smallest, top_value):
    index_at = [jax.random.randint(jax.random.fold_in(rng, axis), (), 0, length) for axis, length in enumerate(entries.shape)]
    longest = entries.shape.index(max(entries.shape))
    next_to = index_at[:longest] + [(index_at[longest] + 1) % entries.shape[longest]] + index_at[longest + 1:]
    return entries.at[tuple(index_at)].set(smallest).at[tuple(next_to)].set(top_value)


def steps_of(own_key, extent, cuts, smallest, largest):
    loudness = 1.0
    for dim, blocks in cuts:
        steps = jax.random.uniform(jax.random.fold_in(jax.random.fold_in(own_key, 6), dim), (blocks,), jnp.float32, smallest / len(cuts), largest / len(cuts))
        loudness = loudness * jnp.repeat(jnp.exp(steps), extent[dim] // blocks).reshape((-1,) + (1,) * (len(extent) - 1 - dim))
    return loudness


def noise(stream_key, shape, spread, most, pieces=(), kind=jnp.bfloat16):
    result = jax.random.normal(stream_key, shape, jnp.float32) * spread
    if len(pieces) > 0:
        result = steps_of(stream_key, shape, pieces, -0.22, 0.18) * result
    return jnp.clip(result, min=-most, max=most).astype(kind)


def setup_inputs(seed: int = 0) -> dict:
    keys = jax.random.split(jax.random.key(seed), 9)
    return {
        "feats": noise(keys[0], (NODES, F), 1.0, 6.0, ((0, 256),)),
        "local_adj": draw_local_adj(jax.random.fold_in(keys[8], 71), 0),
        "bnd_adj": draw_bnd_adj(jax.random.fold_in(keys[8], 71), 0),
        "send_index": touch_ends(jax.random.randint(keys[3], (PARTS_SIZE, ROUNDS, BND), 0, N_LOC), jax.random.fold_in(keys[3], 1), 0, N_LOC - 1).astype(jnp.int32),
        "w_self": noise(keys[4], (F, H), F ** -0.5, 0.5),
        "w_neigh": noise(keys[5], (F, H), 1.0, 4.0),
        "bias": noise(keys[6], (H,), 0.5, 3.0, (), jnp.float32),
        "cotangent": noise(keys[7], (NODES, H), 1.0, 6.0, ((0, 256),)),
    }


def partner_table():
    bits = N_DOM.bit_length() - 1
    table = np.zeros((N_DOM * N_GRP, ROUNDS), np.int32)
    for partition in range(N_DOM * N_GRP):
        dom_index = partition // N_GRP
        grp_index = partition % N_GRP
        for turn in range(ROUNDS):
            table[partition, turn] = (dom_index ^ 1 << bits - 1 - turn % bits) * N_GRP + grp_index
    return table

def reference(feats, local_adj, bnd_adj, send_index, w_self, w_neigh, bias, cotangent):
    parts = N_DOM * N_GRP
    table = jnp.asarray(partner_table())
    feat_blocks = feats.reshape(parts, N_LOC, F)
    adj_blocks = local_adj.reshape(parts, N_LOC, N_LOC)
    cot_blocks = cotangent.reshape(parts, N_LOC, H)

    def forward_one(partition):
        own = feat_blocks[partition]
        adjacency = adj_blocks[partition]
        tiles = bnd_adj[partition]
        summed = jnp.dot(adjacency, own, preferred_element_type=jnp.float32)
        denom = 1.0 + lax.optimization_barrier(jnp.sum(adjacency.astype(jnp.float32), axis=1)) + lax.optimization_barrier(jnp.sum(tiles.astype(jnp.float32), axis=(0, 2)))
        for turn in range(ROUNDS):
            source = table[partition, turn]
            rows = jnp.take(feat_blocks[source], send_index[source, turn], axis=0)
            summed = summed + jnp.dot(tiles[turn], rows, preferred_element_type=jnp.float32)
        agg = (summed / denom[:, None]).astype(jnp.bfloat16)
        pre = jnp.dot(own, w_self, preferred_element_type=jnp.float32) + jnp.dot(agg, w_neigh, preferred_element_type=jnp.float32) + bias
        sigma = jax.nn.sigmoid(pre)
        output = (pre * sigma).astype(jnp.bfloat16)
        slope = sigma * (1.0 + pre * (1.0 - sigma))
        dpre = (cot_blocks[partition].astype(jnp.float32) * slope).astype(jnp.bfloat16)
        dagg = (jnp.dot(dpre, w_neigh.T, preferred_element_type=jnp.float32) / denom[:, None]).astype(jnp.bfloat16)
        back = jnp.einsum('rnb,nf->rbf', tiles.astype(jnp.float32), dagg.astype(jnp.float32)).astype(jnp.bfloat16)
        grad_own = jnp.dot(dpre, w_self.T, preferred_element_type=jnp.float32) + jnp.dot(adjacency.T, dagg, preferred_element_type=jnp.float32)
        part_self = jnp.dot(own.T, dpre, preferred_element_type=jnp.float32)
        part_neigh = jnp.dot(agg.T, dpre, preferred_element_type=jnp.float32)
        return (output, back, grad_own, part_self, part_neigh)
    output, back, grad_own, part_self, part_neigh = lax.map(forward_one, jnp.arange(parts))

    def returns_one(partition):
        total = grad_own[partition]
        for turn in range(ROUNDS):
            source = table[partition, turn]
            total = total.at[send_index[partition, turn]].add(back[source, turn].astype(jnp.float32))
        return total.astype(jnp.bfloat16)
    grad_feats = lax.map(returns_one, jnp.arange(parts))
    scale = 1.0 / math.sqrt(NODES)
    grad_self = lax.optimization_barrier(jnp.sum(part_self, axis=0)) * scale
    grad_neigh = lax.optimization_barrier(jnp.sum(part_neigh, axis=0)) * scale
    return (output.reshape(NODES, H), grad_feats.reshape(NODES, F), grad_self, grad_neigh)
```

```python
import functools
import math

import jax
import jax.numpy as jnp
from jax import lax
from jax.experimental import pallas as pl
from jax.experimental.pallas import tpu as pltpu
from jax.sharding import PartitionSpec as P

F32 = jnp.float32
BF16 = jnp.bfloat16
BLOCK = 256


def dot(left, right, left_dim=1, right_dim=0):
    return lax.dot_general(
        left, right, (((left_dim,), (right_dim,)), ((), ())), preferred_element_type=F32
    )


def whole(shape):
    return pl.BlockSpec(shape, lambda *_: (0,) * len(shape))


def rows_of(block, width):
    return pl.BlockSpec((block, width), lambda i: (i, 0))


def cost(flops, nbytes):
    return pl.CostEstimate(flops=int(flops), bytes_accessed=int(nbytes), transcendentals=0)


def params(mib):
    return pltpu.CompilerParams(vmem_limit_bytes=mib * 1024 * 1024)


def one_hot(index_row, count):
    places = lax.broadcasted_iota(jnp.int32, (count, index_row.shape[1]), 0)
    return (places == index_row).astype(F32).astype(BF16)


def gather_kernel(feats_ref, index_ref, *out_refs):
    turned = feats_ref[...].T
    for turn, out_ref in enumerate(out_refs):
        picked = dot(turned, one_hot(index_ref[turn : turn + 1, :], feats_ref.shape[0]))
        out_ref[...] = picked.T.astype(out_ref.dtype)


def gather_rows(feats, index_lists):
    rounds, picks = index_lists.shape
    rows, width = feats.shape
    shape = jax.ShapeDtypeStruct((picks, width), feats.dtype)
    return pl.pallas_call(
        gather_kernel,
        out_shape=(shape,) * rounds,
        compiler_params=params(32),
        cost_estimate=cost(2 * rows * picks * width * rounds, rows * width * 2),
        name="gather_rows",
    )(feats, index_lists)


def local_kernel(adj_ref, feats_ref, out_ref, wide_ref):
    width = feats_ref.shape[1]

    @pl.when(pl.program_id(0) == 0)
    def _():
        wide_ref[:, :width] = feats_ref[...]
        wide_ref[:, width:] = jnp.ones_like(feats_ref)

    out_ref[...] = dot(adj_ref[...], wide_ref[...])


def local_sum(local_adj, feats):
    rows, width = feats.shape
    return pl.pallas_call(
        local_kernel,
        grid=(rows // BLOCK,),
        in_specs=[rows_of(BLOCK, rows), whole((rows, width))],
        out_specs=rows_of(BLOCK, 2 * width),
        out_shape=jax.ShapeDtypeStruct((rows, 2 * width), F32),
        scratch_shapes=[pltpu.VMEM((rows, 2 * width), BF16)],
        compiler_params=params(32),
        cost_estimate=cost(4 * rows * rows * width, rows * rows * 2),
        name="local_sum",
    )(local_adj, feats)


def middle_kernel(rounds, *refs):
    local_ref, bnd_ref, feats_ref, cot_ref, self_ref, neigh_ref, bias_ref = refs[:7]
    recv_refs = refs[7 : 7 + rounds]
    out_ref, dagg_ref, gself_ref, gw_ref = refs[7 + rounds : 11 + rounds]
    back_refs = refs[11 + rounds : 11 + 2 * rounds]
    wide_ref, back_acc, gw_acc = refs[11 + 2 * rounds :]
    width = feats_ref.shape[1]
    step = pl.program_id(0)

    @pl.when(step == 0)
    def _():
        for turn in range(rounds):
            wide_ref[turn, :, :width] = recv_refs[turn][...]
            wide_ref[turn, :, width:] = jnp.ones_like(recv_refs[turn])
        back_acc[...] = jnp.zeros_like(back_acc)
        gw_acc[...] = jnp.zeros_like(gw_acc)

    total = local_ref[...]
    for turn in range(rounds):
        total = total + dot(bnd_ref[turn], wide_ref[turn])
    inverse = 1.0 / (1.0 + total[:, width:])
    agg = (total[:, :width] * inverse).astype(BF16)
    both = jnp.concatenate([feats_ref[...], agg], axis=1)
    weights = jnp.concatenate([self_ref[...], neigh_ref[...]], axis=0)
    pre = dot(both, weights) + bias_ref[...]
    sig = 1.0 / (1.0 + jnp.exp(-pre))
    out_ref[...] = (pre * sig).astype(out_ref.dtype)
    slope = sig * (1.0 + pre * (1.0 - sig))
    dpre = (cot_ref[...].astype(F32) * slope).astype(BF16)
    grads = dot(dpre, weights, 1, 1)
    gself_ref[...] = grads[:, :width]
    dagg = (grads[:, width:] * inverse).astype(BF16)
    dagg_ref[...] = dagg
    gw_acc[...] += dot(both, dpre, 0, 0)
    turned = dagg.T
    for turn in range(rounds):
        back_acc[turn] += dot(turned, bnd_ref[turn])

    @pl.when(step == pl.num_programs(0) - 1)
    def _():
        gw_ref[...] = gw_acc[...]
        for turn in range(rounds):
            back_refs[turn][...] = back_acc[turn].T.astype(BF16)


def middle(local, bnd_tiles, feats, cotangent, w_self, w_neigh, bias, incoming):
    rounds, rows, bnd = bnd_tiles.shape
    width, hidden = w_self.shape
    results = pl.pallas_call(
        functools.partial(middle_kernel, rounds),
        grid=(rows // BLOCK,),
        in_specs=[
            rows_of(BLOCK, 2 * width),
            pl.BlockSpec((rounds, BLOCK, bnd), lambda i: (0, i, 0)),
            rows_of(BLOCK, width),
            rows_of(BLOCK, hidden),
            whole((width, hidden)),
            whole((width, hidden)),
            whole((1, hidden)),
        ]
        + [whole((bnd, width))] * rounds,
        out_specs=[
            rows_of(BLOCK, hidden),
            rows_of(BLOCK, width),
            rows_of(BLOCK, width),
            whole((2 * width, hidden)),
        ]
        + [whole((bnd, width))] * rounds,
        out_shape=[
            jax.ShapeDtypeStruct((rows, hidden), BF16),
            jax.ShapeDtypeStruct((rows, width), BF16),
            jax.ShapeDtypeStruct((rows, width), F32),
            jax.ShapeDtypeStruct((2 * width, hidden), F32),
        ]
        + [jax.ShapeDtypeStruct((bnd, width), BF16)] * rounds,
        scratch_shapes=[
            pltpu.VMEM((rounds, bnd, 2 * width), BF16),
            pltpu.VMEM((rounds, width, bnd), F32),
            pltpu.VMEM((2 * width, hidden), F32),
        ],
        compiler_params=params(32),
        cost_estimate=cost(8 * rounds * rows * bnd * width, rounds * rows * bnd * 2),
        name="middle",
    )(local, bnd_tiles, feats, cotangent, w_self, w_neigh, bias.reshape(1, hidden), *incoming)
    return results[0], results[1], results[2], results[3], results[4:]


def turned_kernel(adj_ref, dagg_ref, gself_ref, out_ref, acc_ref):
    step = pl.program_id(0)

    @pl.when(step == 0)
    def _():
        acc_ref[...] = jnp.zeros_like(acc_ref)

    acc_ref[...] += dot(dagg_ref[...].T, adj_ref[...])

    @pl.when(step == pl.num_programs(0) - 1)
    def _():
        out_ref[...] = gself_ref[...] + acc_ref[...].T


def turned_sum(local_adj, dagg, gself):
    rows, width = dagg.shape
    return pl.pallas_call(
        turned_kernel,
        grid=(rows // BLOCK,),
        in_specs=[rows_of(BLOCK, rows), rows_of(BLOCK, width), whole((rows, width))],
        out_specs=whole((rows, width)),
        out_shape=jax.ShapeDtypeStruct((rows, width), F32),
        scratch_shapes=[pltpu.VMEM((width, rows), F32)],
        compiler_params=params(32),
        cost_estimate=cost(2 * rows * rows * width, rows * rows * 2),
        name="turned_sum",
    )(local_adj, dagg, gself)


def scatter_kernel(base_ref, index_ref, *refs):
    total = base_ref[...]
    for turn, back_ref in enumerate(refs[:-1]):
        total = total + dot(
            one_hot(index_ref[turn : turn + 1, :], base_ref.shape[0]), back_ref[...]
        )
    refs[-1][...] = total.astype(refs[-1].dtype)


def scatter_rows(base, index_lists, returned):
    rounds, picks = index_lists.shape
    rows, width = base.shape
    return pl.pallas_call(
        scatter_kernel,
        out_shape=jax.ShapeDtypeStruct((rows, width), BF16),
        compiler_params=params(32),
        cost_estimate=cost(2 * rows * picks * width * rounds, rows * width * 6),
        name="scatter_rows",
    )(base, index_lists, *returned)


def swapped(block, axis, distance):
    count = lax.axis_size(axis)
    route = [(low, low ^ 1 << distance) for low in range(count)]
    route = [(low, high) for low, high in route if high < count]
    return lax.ppermute(block, axis, route)


def summed_over_all(partial):
    bits = lax.axis_size("dom").bit_length() - 1
    own = lax.axis_index("grp") == 0
    half = jnp.where(own, partial[0], partial[1])
    other = jnp.where(own, partial[1], partial[0])
    half = half + swapped(other, "grp", 0)
    for bit in range(bits):
        half = half + swapped(half, "dom", bit)
    other = swapped(half, "grp", 0)
    return jnp.where(own, half, other), jnp.where(own, other, half)


def per_device(feats, local_adj, bnd_adj, send_index, w_self, w_neigh, bias, cotangent):
    dom_count = lax.axis_size("dom")
    bit_count = dom_count.bit_length() - 1
    bnd_tiles = bnd_adj[0]
    index_lists = send_index[0]
    rounds = bnd_tiles.shape[0]
    rows, width = feats.shape

    def round_bit(turn):
        return bit_count - 1 - turn % bit_count

    outgoing = gather_rows(feats, index_lists)
    incoming = [swapped(outgoing[turn], "dom", round_bit(turn)) for turn in range(rounds)]
    local = local_sum(local_adj, feats)
    output, dagg, gself, gw, back = middle(
        local, bnd_tiles, feats, cotangent, w_self, w_neigh, bias, incoming
    )
    returned = [swapped(back[turn], "dom", round_bit(turn)) for turn in range(rounds)]
    base = turned_sum(local_adj, dagg, gself)
    grad_feats = scatter_rows(base, index_lists, returned)
    sum_self, sum_neigh = summed_over_all(gw.reshape(2, width, gw.shape[1]))
    scale = 1.0 / math.sqrt(rows * dom_count * lax.axis_size("grp"))
    return output, grad_feats, sum_self * scale, sum_neigh * scale


def solution(mesh):
    placed = (
        P(("dom", "grp"), None),
        P(("dom", "grp"), None),
        P(("dom", "grp"), None, None, None),
        P(("dom", "grp"), None, None),
        P(),
        P(),
        P(),
        P(("dom", "grp"), None),
    )
    return jax.shard_map(
        per_device,
        mesh=mesh,
        in_specs=placed,
        out_specs=(P(("dom", "grp"), None), P(("dom", "grp"), None), P(), P()),
        check_vma=False,
    )
```

```python
import functools
import math

import jax
import jax.numpy as jnp
from jax import lax
from jax.experimental import pallas as pl
from jax.experimental.pallas import tpu as pltpu
from jax.sharding import Mesh
from jax.sharding import PartitionSpec as P

F32 = jnp.float32
BF16 = jnp.bfloat16
BLOCK = 384
SIDE = 4
AXES = ("z", "y", "x", "core")
PLANE = AXES[1:]


def dot(left, right, left_dim=1, right_dim=0):
    return lax.dot_general(
        left, right, (((left_dim,), (right_dim,)), ((), ())), preferred_element_type=F32
    )


def cost(flops, nbytes):
    return pl.CostEstimate(flops=int(flops), bytes_accessed=int(nbytes), transcendentals=0)


def params(mib):
    return pltpu.CompilerParams(vmem_limit_bytes=mib * 1024 * 1024)


def one_hot(index_row, count):
    places = lax.broadcasted_iota(jnp.int32, (count, index_row.shape[1]), 0)
    return (places == index_row).astype(F32).astype(BF16)


def in_hbm(array):
    return pltpu.with_memory_space_constraint(array, pltpu.HBM)


ANY = pl.BlockSpec(memory_space=pl.ANY)
VMEM = pl.BlockSpec(memory_space=pltpu.VMEM)
DMA = pltpu.SemaphoreType.DMA


def gather_kernel(rounds, feats_hbm, index_hbm, adj_hbm, *refs):
    out_refs, (wide_ref, adj_ref, index_ref, sems) = refs[:rounds], refs[rounds:]
    rows, width = feats_hbm.shape
    copies = [
        pltpu.make_async_copy(index_hbm, index_ref, sems.at[0]),
        pltpu.make_async_copy(feats_hbm, wide_ref.at[:, pl.ds(0, width)], sems.at[1]),
        pltpu.make_async_copy(adj_hbm, adj_ref, sems.at[2]),
    ]
    for copy in copies:
        copy.start()
    wide_ref[:, width:] = jnp.ones((rows, width), BF16)
    copies[0].wait()
    copies[1].wait()
    turned = wide_ref[:, :width].T
    for turn, out_ref in enumerate(out_refs):
        out_ref[...] = dot(turned, one_hot(index_ref[turn], rows)).T.astype(BF16)
    copies[2].wait()


def gather_rows(feats, index_lists, local_adj):
    rounds, _, picks = index_lists.shape
    rows, width = feats.shape
    results = pl.pallas_call(
        functools.partial(gather_kernel, rounds),
        in_specs=[ANY, ANY, ANY],
        out_specs=[VMEM] * (rounds + 2),
        out_shape=[jax.ShapeDtypeStruct((picks, width), BF16)] * rounds
        + [pltpu.VMEM((rows, 2 * width), BF16), pltpu.VMEM(local_adj.shape, BF16)],
        scratch_shapes=[pltpu.VMEM(index_lists.shape, jnp.int32), DMA((3,))],
        compiler_params=params(24),
        cost_estimate=cost(2 * rows * picks * width * rounds, rows * width * 2),
        name="gather_rows",
    )(in_hbm(feats), in_hbm(index_lists), in_hbm(local_adj))
    return results[:rounds], results[rounds], results[rounds + 1]


def local_kernel(adj_ref, wide_ref, out_ref):
    for start in range(0, adj_ref.shape[0], BLOCK):
        span = slice(start, start + BLOCK)
        out_ref[span, :] = dot(adj_ref[span, :], wide_ref[...])


def local_sum(local_adj, wide):
    rows = local_adj.shape[0]
    return pl.pallas_call(
        local_kernel,
        out_shape=jax.ShapeDtypeStruct(wide.shape, F32),
        compiler_params=params(16),
        cost_estimate=cost(2 * rows * rows * wide.shape[1], rows * rows * 2),
        name="local_sum",
    )(local_adj, wide)


def middle_kernel(rounds, *refs):
    local_ref, bnd_ref, feats_ref, cot_ref, self_ref, neigh_ref, bias_ref = refs[:7]
    recv_refs = refs[7 : 7 + rounds]
    out_hbm, dagg_ref, gself_ref, gw_hbm = refs[7 + rounds : 11 + rounds]
    back_refs = refs[11 + rounds : 11 + 2 * rounds]
    wide_ref, both_ref, dpre_ref, inverse_ref, out_ref, gw_ref, sems = refs[11 + 2 * rounds :]
    rows, width = dagg_ref.shape
    bnd = bnd_ref.shape[2]
    spans = [slice(start, start + BLOCK) for start in range(0, rows, BLOCK)]

    for turn in range(rounds):
        span = slice(turn * bnd, (turn + 1) * bnd)
        wide_ref[span, :width] = recv_refs[turn][...]
        wide_ref[span, width:] = jnp.ones_like(recv_refs[turn])
    both_ref[:, :width] = feats_ref[:, :width]
    for span in spans:
        tiles = jnp.concatenate([bnd_ref[turn, span, :] for turn in range(rounds)], axis=1)
        total = local_ref[span, :] + dot(tiles, wide_ref[...])
        inverse = 1.0 / (1.0 + total[:, width:])
        inverse_ref[span, :] = inverse
        both_ref[span, width:] = (total[:, :width] * inverse).astype(BF16)

    weights = jnp.concatenate([self_ref[...], neigh_ref[...]], axis=0)
    for span in spans:
        pre = dot(both_ref[span, :], weights) + bias_ref[...]
        sig = 0.5 + 0.5 * jnp.tanh(0.5 * pre)
        out = pre * sig
        out_ref[span, :] = out.astype(BF16)
        slope = sig * (1.0 + (pre - out))
        dpre_ref[span, :] = (cot_ref[span, :].astype(F32) * slope).astype(BF16)

    gw = dot(both_ref[...], dpre_ref[...], 0, 0).astype(BF16)
    for half in range(gw.shape[1] // width):
        gw_ref[half] = gw[:, half * width : (half + 1) * width]
    gw_copy = pltpu.make_async_copy(gw_ref, gw_hbm, sems.at[0])
    gw_copy.start()
    out_copy = pltpu.make_async_copy(out_ref, out_hbm, sems.at[1])
    out_copy.start()

    for span in spans:
        grads = dot(dpre_ref[span, :], weights, 1, 1)
        gself_ref[span, :] = grads[:, :width]
        dagg_ref[span, :] = (grads[:, width:] * inverse_ref[span, :]).astype(BF16)

    turned = dagg_ref[...].T
    for turn in range(rounds):
        back_refs[turn][...] = dot(turned, bnd_ref[turn]).T.astype(BF16)
    gw_copy.wait()
    out_copy.wait()


def middle(local, bnd_tiles, wide, cotangent, w_self, w_neigh, bias, incoming):
    rounds, rows, bnd = bnd_tiles.shape
    width, hidden = w_self.shape
    results = pl.pallas_call(
        functools.partial(middle_kernel, rounds),
        in_specs=[VMEM] * (7 + rounds),
        out_specs=[ANY, VMEM, VMEM, ANY] + [VMEM] * rounds,
        out_shape=[
            pltpu.HBM((rows, hidden), BF16),
            jax.ShapeDtypeStruct((rows, width), BF16),
            jax.ShapeDtypeStruct((rows, width), F32),
            pltpu.HBM((hidden // width, 2 * width, width), BF16),
        ]
        + [jax.ShapeDtypeStruct((bnd, width), BF16)] * rounds,
        scratch_shapes=[
            pltpu.VMEM((rounds * bnd, 2 * width), BF16),
            pltpu.VMEM((rows, 2 * width), BF16),
            pltpu.VMEM((rows, hidden), BF16),
            pltpu.VMEM((rows, width), F32),
            pltpu.VMEM((rows, hidden), BF16),
            pltpu.VMEM((hidden // width, 2 * width, width), BF16),
            DMA((2,)),
        ],
        compiler_params=params(32),
        cost_estimate=cost(8 * rounds * rows * bnd * width, rounds * rows * bnd * 2),
        name="middle",
    )(
        local,
        bnd_tiles,
        wide,
        cotangent,
        w_self,
        w_neigh,
        bias.reshape(1, hidden),
        *incoming,
    )
    return results[0], results[1], results[2], results[3], results[4:]


def turned_kernel(adj_ref, dagg_ref, gself_ref, out_ref):
    out_ref[...] = gself_ref[...] + dot(dagg_ref[...].T, adj_ref[...]).T


def turned_sum(local_adj, dagg, gself):
    rows, width = dagg.shape
    return pl.pallas_call(
        turned_kernel,
        out_shape=jax.ShapeDtypeStruct((rows, width), F32),
        compiler_params=params(32),
        cost_estimate=cost(2 * rows * rows * width, rows * rows * 2),
        name="turned_sum",
    )(local_adj, dagg, gself)


def spread_kernel(scale, parts_ref, out_hbm, wide_ref, sem):
    total = parts_ref[0].astype(F32)
    for number in range(1, parts_ref.shape[0]):
        total = total + parts_ref[number].astype(F32)
    total = (total * scale).astype(wide_ref.dtype)
    for number in range(wide_ref.shape[0]):
        wide_ref[number] = total
    copy = pltpu.make_async_copy(wide_ref, out_hbm, sem)
    copy.start()
    copy.wait()


def sum_and_spread(parts, copies, dtype, scale):
    shape = (copies,) + parts.shape[1:]
    return pl.pallas_call(
        functools.partial(spread_kernel, scale),
        in_specs=[VMEM],
        out_specs=ANY,
        out_shape=pltpu.HBM(shape, dtype),
        scratch_shapes=[pltpu.VMEM(shape, dtype), DMA(())],
        compiler_params=params(16),
        name="sum_and_spread",
    )(parts)


def scatter_kernel(base_ref, index_ref, *refs):
    total = base_ref[...]
    for turn, back_ref in enumerate(refs[:-1]):
        total = total + dot(one_hot(index_ref[turn], base_ref.shape[0]), back_ref[...])
    refs[-1][...] = total.astype(refs[-1].dtype)


def scatter_rows(base, index_lists, returned):
    rounds, _, picks = index_lists.shape
    rows, width = base.shape
    return pl.pallas_call(
        scatter_kernel,
        out_shape=jax.ShapeDtypeStruct((rows, width), BF16),
        compiler_params=params(32),
        cost_estimate=cost(2 * rows * picks * width * rounds, rows * width * 6),
        name="scatter_rows",
    )(base, index_lists, *returned)


def swapped(block, bit):
    count = math.prod(lax.axis_size(axis) for axis in AXES)
    return lax.ppermute(block, AXES, [(low, low ^ 1 << bit) for low in range(count)])


def after(value, *others):
    return lax.optimization_barrier((value, *others))[0]


def per_device(feats, local_adj, bnd_adj, send_index, w_self, w_neigh, bias, cotangent):
    chips = math.prod(lax.axis_size(axis) for axis in AXES[:-1])
    cores = lax.axis_size(AXES[-1])
    bits = chips.bit_length() - 1
    bnd_tiles = bnd_adj[0]
    rounds, _, picks = bnd_tiles.shape
    index_lists = send_index.reshape(rounds, 1, -1)
    rows, width = feats.shape

    def partner(turn):
        return bits - turn % bits

    outgoing, wide, near_adj = gather_rows(feats, index_lists, local_adj)
    incoming = [swapped(outgoing[turn], partner(turn)) for turn in range(rounds)]
    local = local_sum(near_adj, wide)
    output, dagg, gself, gw, back = middle(
        local, bnd_tiles, wide, cotangent, w_self, w_neigh, bias, incoming
    )
    base = turned_sum(local_adj, dagg, gself)

    plane = math.prod(lax.axis_size(axis) for axis in PLANE)
    planes = chips * cores // plane
    pieces = gw.reshape(plane, -1, width)
    pieces = lax.all_to_all(pieces, PLANE, 0, 0, tiled=True)
    near = [turn for turn in range(rounds) if partner(turn) < plane.bit_length() - 1]
    far = [turn for turn in range(rounds) if turn not in near]
    returned = {turn: swapped(back[turn], partner(turn)) for turn in far}
    pieces = sum_and_spread(pieces, planes, F32, 1.0)
    pieces = after(pieces, *[returned[turn] for turn in far])
    pieces = lax.all_to_all(pieces, AXES[:1], 0, 0, tiled=True)
    returned |= {turn: swapped(back[turn], partner(turn)) for turn in near}
    scale = 1.0 / math.sqrt(rows * chips * cores)
    pieces = sum_and_spread(pieces, plane, BF16, scale)
    pieces = after(pieces, *[returned[turn] for turn in near])
    pieces = lax.all_to_all(pieces, PLANE, 0, 0, tiled=True)
    grad_feats = scatter_rows(base, index_lists, [returned[turn] for turn in range(rounds)])
    sums = jnp.concatenate([*pieces.reshape(gw.shape)], axis=1).astype(F32)
    return output, grad_feats, sums[:width], sums[width:]


def solution(mesh):
    chips = mesh.shape["dom"] // SIDE**2
    shape = (chips, SIDE, SIDE, mesh.shape["grp"])
    mesh = Mesh(mesh.devices.reshape(shape), AXES)
    placed = (
        P(AXES, None),
        P(AXES, None),
        P(AXES, None, None, None),
        P(AXES, None, None),
        P(),
        P(),
        P(),
        P(AXES, None),
    )
    return jax.shard_map(
        per_device,
        mesh=mesh,
        in_specs=placed,
        out_specs=(P(AXES, None), P(AXES, None), P(), P()),
        check_vma=False,
    )
```

```python
import functools
import math

import jax
import jax.numpy as jnp
from jax import lax
from jax.experimental import pallas as pl
from jax.experimental.pallas import tpu as pltpu
from jax.sharding import Mesh
from jax.sharding import PartitionSpec as P

F32 = jnp.float32
BF16 = jnp.bfloat16
BLOCK = 384
ORDER = (2, 3, 0, 1, 5, 4)
EARLY = 2
SIDE = 4
AXES = ("z", "y", "x", "core")
PLANE = AXES[1:]


def dot(left, right, left_dim=1, right_dim=0):
    return lax.dot_general(
        left, right, (((left_dim,), (right_dim,)), ((), ())), preferred_element_type=F32
    )


def cost(flops, nbytes):
    return pl.CostEstimate(flops=int(flops), bytes_accessed=int(nbytes), transcendentals=0)


def params(mib):
    return pltpu.CompilerParams(vmem_limit_bytes=mib * 1024 * 1024)


def one_hot(index_row, count):
    places = lax.broadcasted_iota(jnp.int32, (count, index_row.shape[1]), 0)
    return (places == index_row).astype(F32).astype(BF16)


def in_hbm(array):
    return pltpu.with_memory_space_constraint(array, pltpu.HBM)


ANY = pl.BlockSpec(memory_space=pl.ANY)
VMEM = pl.BlockSpec(memory_space=pltpu.VMEM)
DMA = pltpu.SemaphoreType.DMA


def gather_kernel(rounds, feats_hbm, index_hbm, adj_hbm, *refs):
    out_refs, (wide_ref, adj_ref, index_ref, sems) = refs[:rounds], refs[rounds:]
    rows, width = feats_hbm.shape
    copies = [
        pltpu.make_async_copy(index_hbm, index_ref, sems.at[0]),
        pltpu.make_async_copy(feats_hbm, wide_ref.at[:, pl.ds(0, width)], sems.at[1]),
        pltpu.make_async_copy(adj_hbm, adj_ref, sems.at[2]),
    ]
    for copy in copies:
        copy.start()
    wide_ref[:, width:] = jnp.ones((rows, width), BF16)
    copies[0].wait()
    copies[1].wait()
    turned = wide_ref[:, :width].T
    for turn, out_ref in enumerate(out_refs):
        out_ref[...] = dot(turned, one_hot(index_ref[turn], rows)).T.astype(BF16)
    copies[2].wait()


def gather_rows(feats, index_lists, local_adj):
    rounds, _, picks = index_lists.shape
    rows, width = feats.shape
    results = pl.pallas_call(
        functools.partial(gather_kernel, rounds),
        in_specs=[ANY, ANY, ANY],
        out_specs=[VMEM] * (rounds + 2),
        out_shape=[jax.ShapeDtypeStruct((picks, width), BF16)] * rounds
        + [pltpu.VMEM((rows, 2 * width), BF16), pltpu.VMEM(local_adj.shape, BF16)],
        scratch_shapes=[pltpu.VMEM(index_lists.shape, jnp.int32), DMA((3,))],
        compiler_params=params(24),
        cost_estimate=cost(2 * rows * picks * width * rounds, rows * width * 2),
        name="gather_rows",
    )(in_hbm(feats), in_hbm(index_lists), in_hbm(local_adj))
    return results[:rounds], results[rounds], results[rounds + 1]


def widen(wide_ref, recv_refs):
    picks, width = recv_refs[0].shape
    for number, recv_ref in enumerate(recv_refs):
        span = slice(number * picks, (number + 1) * picks)
        wide_ref[span, :width] = recv_ref[...]
        wide_ref[span, width:] = jnp.ones((picks, width), BF16)


def tiles_of(bnd_ref, span, turns):
    return jnp.concatenate([bnd_ref[turn, span, :] for turn in turns], axis=1)


def early_kernel(turns, adj_ref, wide_ref, bnd_ref, *refs):
    recv_refs, (out_ref, recv_wide_ref) = refs[: len(turns)], refs[len(turns) :]
    widen(recv_wide_ref, recv_refs)
    for start in range(0, adj_ref.shape[0], BLOCK):
        span = slice(start, start + BLOCK)
        total = dot(adj_ref[span, :], wide_ref[...])
        out_ref[span, :] = total + dot(tiles_of(bnd_ref, span, turns), recv_wide_ref[...])


def early_sum(local_adj, wide, bnd_tiles, turns, incoming):
    rows, picks = local_adj.shape[0], bnd_tiles.shape[2]
    return pl.pallas_call(
        functools.partial(early_kernel, turns),
        out_shape=jax.ShapeDtypeStruct(wide.shape, F32),
        scratch_shapes=[pltpu.VMEM((len(turns) * picks, wide.shape[1]), BF16)],
        compiler_params=params(16),
        cost_estimate=cost(2 * rows * rows * wide.shape[1], rows * rows * 2),
        name="early_sum",
    )(local_adj, wide, bnd_tiles, *incoming)


def middle_kernel(turns, *refs):
    local_ref, bnd_ref, feats_ref, cot_ref, self_ref, neigh_ref, bias_ref = refs[:7]
    rounds = bnd_ref.shape[0]
    recv_refs, refs = refs[7 : 7 + len(turns)], refs[7 + len(turns) :]
    out_hbm, dagg_ref, gself_ref, gw_hbm = refs[:4]
    back_refs = refs[4 : 4 + rounds]
    wide_ref, both_ref, dpre_ref, inverse_ref, out_ref, gw_ref, sems = refs[4 + rounds :]
    rows, width = dagg_ref.shape
    spans = [slice(start, start + BLOCK) for start in range(0, rows, BLOCK)]

    widen(wide_ref, recv_refs)
    both_ref[:, :width] = feats_ref[:, :width]
    for span in spans:
        total = local_ref[span, :] + dot(tiles_of(bnd_ref, span, turns), wide_ref[...])
        inverse = 1.0 / (1.0 + total[:, width:])
        inverse_ref[span, :] = inverse
        both_ref[span, width:] = (total[:, :width] * inverse).astype(BF16)

    weights = jnp.concatenate([self_ref[...], neigh_ref[...]], axis=0)
    for span in spans:
        pre = dot(both_ref[span, :], weights) + bias_ref[...]
        sig = 0.5 + 0.5 * jnp.tanh(0.5 * pre)
        out = pre * sig
        out_ref[span, :] = out.astype(BF16)
        slope = sig * (1.0 + (pre - out))
        dpre_ref[span, :] = (cot_ref[span, :].astype(F32) * slope).astype(BF16)

    gw = dot(both_ref[...], dpre_ref[...], 0, 0).astype(BF16)
    for half in range(gw.shape[1] // width):
        gw_ref[half] = gw[:, half * width : (half + 1) * width]
    gw_copy = pltpu.make_async_copy(gw_ref, gw_hbm, sems.at[0])
    gw_copy.start()
    out_copy = pltpu.make_async_copy(out_ref, out_hbm, sems.at[1])
    out_copy.start()

    for span in spans:
        grads = dot(dpre_ref[span, :], weights, 1, 1)
        gself_ref[span, :] = grads[:, :width]
        dagg_ref[span, :] = (grads[:, width:] * inverse_ref[span, :]).astype(BF16)

    turned = dagg_ref[...].T
    for turn in range(rounds):
        back_refs[turn][...] = dot(turned, bnd_ref[turn]).T.astype(BF16)
    gw_copy.wait()
    out_copy.wait()


def middle(local, bnd_tiles, wide, cotangent, w_self, w_neigh, bias, turns, incoming):
    rounds, rows, bnd = bnd_tiles.shape
    width, hidden = w_self.shape
    results = pl.pallas_call(
        functools.partial(middle_kernel, turns),
        in_specs=[VMEM] * (7 + len(turns)),
        out_specs=[ANY, VMEM, VMEM, ANY] + [VMEM] * rounds,
        out_shape=[
            pltpu.HBM((rows, hidden), BF16),
            jax.ShapeDtypeStruct((rows, width), BF16),
            jax.ShapeDtypeStruct((rows, width), F32),
            pltpu.HBM((hidden // width, 2 * width, width), BF16),
        ]
        + [jax.ShapeDtypeStruct((bnd, width), BF16)] * rounds,
        scratch_shapes=[
            pltpu.VMEM((len(turns) * bnd, 2 * width), BF16),
            pltpu.VMEM((rows, 2 * width), BF16),
            pltpu.VMEM((rows, hidden), BF16),
            pltpu.VMEM((rows, width), F32),
            pltpu.VMEM((rows, hidden), BF16),
            pltpu.VMEM((hidden // width, 2 * width, width), BF16),
            DMA((2,)),
        ],
        compiler_params=params(32),
        cost_estimate=cost(8 * rounds * rows * bnd * width, rounds * rows * bnd * 2),
        name="middle",
    )(
        local,
        bnd_tiles,
        wide,
        cotangent,
        w_self,
        w_neigh,
        bias.reshape(1, hidden),
        *incoming,
    )
    return results[0], results[1], results[2], results[3], results[4:]


def turned_kernel(adj_ref, dagg_ref, gself_ref, out_ref):
    out_ref[...] = gself_ref[...] + dot(dagg_ref[...].T, adj_ref[...]).T


def turned_sum(local_adj, dagg, gself):
    rows, width = dagg.shape
    return pl.pallas_call(
        turned_kernel,
        out_shape=jax.ShapeDtypeStruct((rows, width), F32),
        compiler_params=params(32),
        cost_estimate=cost(2 * rows * rows * width, rows * rows * 2),
        name="turned_sum",
    )(local_adj, dagg, gself)


def spread_kernel(scale, parts_ref, out_hbm, wide_ref, sem):
    total = parts_ref[0].astype(F32)
    for number in range(1, parts_ref.shape[0]):
        total = total + parts_ref[number].astype(F32)
    total = (total * scale).astype(wide_ref.dtype)
    for number in range(wide_ref.shape[0]):
        wide_ref[number] = total
    copy = pltpu.make_async_copy(wide_ref, out_hbm, sem)
    copy.start()
    copy.wait()


def sum_and_spread(parts, copies, dtype, scale):
    shape = (copies,) + parts.shape[1:]
    return pl.pallas_call(
        functools.partial(spread_kernel, scale),
        in_specs=[VMEM],
        out_specs=ANY,
        out_shape=pltpu.HBM(shape, dtype),
        scratch_shapes=[pltpu.VMEM(shape, dtype), DMA(())],
        compiler_params=params(16),
        name="sum_and_spread",
    )(parts)


def scatter_kernel(base_ref, index_ref, *refs):
    total = base_ref[...]
    for turn, back_ref in enumerate(refs[:-1]):
        total = total + dot(one_hot(index_ref[turn], base_ref.shape[0]), back_ref[...])
    refs[-1][...] = total.astype(refs[-1].dtype)


def scatter_rows(base, index_lists, returned):
    rounds, _, picks = index_lists.shape
    rows, width = base.shape
    return pl.pallas_call(
        scatter_kernel,
        out_shape=jax.ShapeDtypeStruct((rows, width), BF16),
        compiler_params=params(32),
        cost_estimate=cost(2 * rows * picks * width * rounds, rows * width * 6),
        name="scatter_rows",
    )(base, index_lists, *returned)


def swapped(block, bit):
    count = math.prod(lax.axis_size(axis) for axis in AXES)
    return lax.ppermute(block, AXES, [(low, low ^ 1 << bit) for low in range(count)])


def after(value, *others):
    return lax.optimization_barrier((value, *others))[0]


def per_device(feats, local_adj, bnd_adj, send_index, w_self, w_neigh, bias, cotangent):
    chips = math.prod(lax.axis_size(axis) for axis in AXES[:-1])
    cores = lax.axis_size(AXES[-1])
    bits = chips.bit_length() - 1
    bnd_tiles = bnd_adj[0]
    rounds, _, picks = bnd_tiles.shape
    index_lists = send_index.reshape(rounds, 1, -1)
    rows, width = feats.shape

    def partner(turn):
        return bits - turn % bits

    outgoing, wide, near_adj = gather_rows(feats, index_lists, local_adj)
    incoming = [swapped(outgoing[turn], partner(turn)) for turn in ORDER]
    first, last = ORDER[:EARLY], ORDER[EARLY:]
    local = early_sum(near_adj, wide, bnd_tiles, first, incoming[:EARLY])
    output, dagg, gself, gw, back = middle(
        local, bnd_tiles, wide, cotangent, w_self, w_neigh, bias, last, incoming[EARLY:]
    )

    plane = math.prod(lax.axis_size(axis) for axis in PLANE)
    planes = chips * cores // plane
    pieces = gw.reshape(plane, -1, width)
    pieces = lax.all_to_all(pieces, PLANE, 0, 0, tiled=True)
    far = (2, 0, 4)
    near = (1, 3, 5)
    returned = {turn: swapped(back[turn], partner(turn)) for turn in far}
    pieces = sum_and_spread(pieces, planes, F32, 1.0)
    pieces = lax.all_to_all(pieces, AXES[:1], 0, 0, tiled=True)
    for turn in near:
        returned[turn] = swapped(after(back[turn], *[returned[other] for other in far]), partner(turn))
    scale = 1.0 / math.sqrt(rows * chips * cores)
    pieces = sum_and_spread(pieces, plane, BF16, scale)
    pieces = lax.all_to_all(pieces, PLANE, 0, 0, tiled=True)
    base = turned_sum(local_adj, after(dagg, *[returned[turn] for turn in near]), gself)
    grad_feats = scatter_rows(base, index_lists, [returned[turn] for turn in range(rounds)])
    sums = jnp.concatenate([*pieces.reshape(gw.shape)], axis=1).astype(F32)
    return output, grad_feats, sums[:width], sums[width:]


def solution(mesh):
    chips = mesh.shape["dom"] // SIDE**2
    shape = (chips, SIDE, SIDE, mesh.shape["grp"])
    mesh = Mesh(mesh.devices.reshape(shape), AXES)
    placed = (
        P(AXES, None),
        P(AXES, None),
        P(AXES, None, None, None),
        P(AXES, None, None),
        P(),
        P(),
        P(),
        P(AXES, None),
    )
    return jax.shard_map(
        per_device,
        mesh=mesh,
        in_specs=placed,
        out_specs=(P(AXES, None), P(AXES, None), P(), P()),
        check_vma=False,
    )
```

```python
import functools
import math

import jax
import jax.numpy as jnp
from jax import lax
from jax.experimental import pallas as pl
from jax.experimental.pallas import tpu as pltpu
from jax.sharding import Mesh
from jax.sharding import PartitionSpec as P

F32 = jnp.float32
BF16 = jnp.bfloat16
BLOCK = 384
ORDER = (2, 3, 1, 0, 5, 4)
EARLY = 3
SIDE = 4
AXES = ("z", "y", "x", "core")
PLANE = AXES[1:]


def dot(left, right, left_dim=1, right_dim=0):
    return lax.dot_general(
        left, right, (((left_dim,), (right_dim,)), ((), ())), preferred_element_type=F32
    )


def cost(flops, nbytes):
    return pl.CostEstimate(flops=int(flops), bytes_accessed=int(nbytes), transcendentals=0)


def params(mib):
    return pltpu.CompilerParams(vmem_limit_bytes=mib * 1024 * 1024)


def one_hot(index_row, count):
    places = lax.broadcasted_iota(jnp.int32, (count, index_row.shape[1]), 0)
    return (places == index_row).astype(F32).astype(BF16)


def in_hbm(array):
    return pltpu.with_memory_space_constraint(array, pltpu.HBM)


ANY = pl.BlockSpec(memory_space=pl.ANY)
VMEM = pl.BlockSpec(memory_space=pltpu.VMEM)
DMA = pltpu.SemaphoreType.DMA


def gather_kernel(rounds, feats_hbm, index_hbm, adj_hbm, *refs):
    out_refs, (wide_ref, adj_ref, index_ref, sems) = refs[:rounds], refs[rounds:]
    rows, width = feats_hbm.shape
    copies = [
        pltpu.make_async_copy(index_hbm, index_ref, sems.at[0]),
        pltpu.make_async_copy(feats_hbm, wide_ref.at[:, pl.ds(0, width)], sems.at[1]),
        pltpu.make_async_copy(adj_hbm, adj_ref, sems.at[2]),
    ]
    for copy in copies:
        copy.start()
    wide_ref[:, width:] = jnp.ones((rows, width), BF16)
    copies[0].wait()
    copies[1].wait()
    turned = wide_ref[:, :width].T
    for turn, out_ref in enumerate(out_refs):
        out_ref[...] = dot(turned, one_hot(index_ref[turn], rows)).T.astype(BF16)
    copies[2].wait()


def gather_rows(feats, index_lists, local_adj):
    rounds, _, picks = index_lists.shape
    rows, width = feats.shape
    results = pl.pallas_call(
        functools.partial(gather_kernel, rounds),
        in_specs=[ANY, ANY, ANY],
        out_specs=[VMEM] * (rounds + 2),
        out_shape=[jax.ShapeDtypeStruct((picks, width), BF16)] * rounds
        + [pltpu.VMEM((rows, 2 * width), BF16), pltpu.VMEM(local_adj.shape, BF16)],
        scratch_shapes=[pltpu.VMEM(index_lists.shape, jnp.int32), DMA((3,))],
        compiler_params=params(24),
        cost_estimate=cost(2 * rows * picks * width * rounds, rows * width * 2),
        name="gather_rows",
    )(in_hbm(feats), in_hbm(index_lists), in_hbm(local_adj))
    return results[:rounds], results[rounds], results[rounds + 1]


def widen(wide_ref, recv_refs):
    picks, width = recv_refs[0].shape
    for number, recv_ref in enumerate(recv_refs):
        span = slice(number * picks, (number + 1) * picks)
        wide_ref[span, :width] = recv_ref[...]
        wide_ref[span, width:] = jnp.ones((picks, width), BF16)


def tiles_of(bnd_ref, span, turns):
    return jnp.concatenate([bnd_ref[turn, span, :] for turn in turns], axis=1)


def early_kernel(turns, adj_ref, wide_ref, bnd_ref, *refs):
    recv_refs, (out_ref, recv_wide_ref) = refs[: len(turns)], refs[len(turns) :]
    widen(recv_wide_ref, recv_refs)
    for start in range(0, adj_ref.shape[0], BLOCK):
        span = slice(start, start + BLOCK)
        total = dot(adj_ref[span, :], wide_ref[...])
        out_ref[span, :] = total + dot(tiles_of(bnd_ref, span, turns), recv_wide_ref[...])


def early_sum(local_adj, wide, bnd_tiles, turns, incoming):
    rows, picks = local_adj.shape[0], bnd_tiles.shape[2]
    return pl.pallas_call(
        functools.partial(early_kernel, turns),
        out_shape=jax.ShapeDtypeStruct(wide.shape, F32),
        scratch_shapes=[pltpu.VMEM((len(turns) * picks, wide.shape[1]), BF16)],
        compiler_params=params(16),
        cost_estimate=cost(2 * rows * rows * wide.shape[1], rows * rows * 2),
        name="early_sum",
    )(local_adj, wide, bnd_tiles, *incoming)


def middle_kernel(turns, *refs):
    local_ref, bnd_ref, feats_ref, cot_ref, self_ref, neigh_ref, bias_ref = refs[:7]
    rounds = bnd_ref.shape[0]
    recv_refs, refs = refs[7 : 7 + len(turns)], refs[7 + len(turns) :]
    out_hbm, dagg_ref, gself_ref, gw_hbm = refs[:4]
    back_refs = refs[4 : 4 + rounds]
    wide_ref, both_ref, dpre_ref, inverse_ref, out_ref, gw_ref, sems = refs[4 + rounds :]
    rows, width = dagg_ref.shape
    spans = [slice(start, start + BLOCK) for start in range(0, rows, BLOCK)]

    widen(wide_ref, recv_refs)
    both_ref[:, :width] = feats_ref[:, :width]
    for span in spans:
        total = local_ref[span, :] + dot(tiles_of(bnd_ref, span, turns), wide_ref[...])
        inverse = 1.0 / (1.0 + total[:, width:])
        inverse_ref[span, :] = inverse
        both_ref[span, width:] = (total[:, :width] * inverse).astype(BF16)

    weights = jnp.concatenate([self_ref[...], neigh_ref[...]], axis=0)
    for span in spans:
        pre = dot(both_ref[span, :], weights) + bias_ref[...]
        sig = 0.5 + 0.5 * jnp.tanh(0.5 * pre)
        out = pre * sig
        out_ref[span, :] = out.astype(BF16)
        slope = sig * (1.0 + (pre - out))
        dpre_ref[span, :] = (cot_ref[span, :].astype(F32) * slope).astype(BF16)

    gw = dot(both_ref[...], dpre_ref[...], 0, 0).astype(BF16)
    for half in range(gw.shape[1] // width):
        gw_ref[half] = gw[:, half * width : (half + 1) * width]
    gw_copy = pltpu.make_async_copy(gw_ref, gw_hbm, sems.at[0])
    gw_copy.start()
    out_copy = pltpu.make_async_copy(out_ref, out_hbm, sems.at[1])
    out_copy.start()

    for span in spans:
        grads = dot(dpre_ref[span, :], weights, 1, 1)
        gself_ref[span, :] = grads[:, :width]
        dagg_ref[span, :] = (grads[:, width:] * inverse_ref[span, :]).astype(BF16)

    turned = dagg_ref[...].T
    for turn in range(rounds):
        back_refs[turn][...] = dot(turned, bnd_ref[turn]).T.astype(BF16)
    gw_copy.wait()
    out_copy.wait()


def middle(local, bnd_tiles, wide, cotangent, w_self, w_neigh, bias, turns, incoming):
    rounds, rows, bnd = bnd_tiles.shape
    width, hidden = w_self.shape
    results = pl.pallas_call(
        functools.partial(middle_kernel, turns),
        in_specs=[VMEM] * (7 + len(turns)),
        out_specs=[ANY, VMEM, VMEM, ANY] + [VMEM] * rounds,
        out_shape=[
            pltpu.HBM((rows, hidden), BF16),
            jax.ShapeDtypeStruct((rows, width), BF16),
            jax.ShapeDtypeStruct((rows, width), F32),
            pltpu.HBM((hidden // width, 2 * width, width), BF16),
        ]
        + [jax.ShapeDtypeStruct((bnd, width), BF16)] * rounds,
        scratch_shapes=[
            pltpu.VMEM((len(turns) * bnd, 2 * width), BF16),
            pltpu.VMEM((rows, 2 * width), BF16),
            pltpu.VMEM((rows, hidden), BF16),
            pltpu.VMEM((rows, width), F32),
            pltpu.VMEM((rows, hidden), BF16),
            pltpu.VMEM((hidden // width, 2 * width, width), BF16),
            DMA((2,)),
        ],
        compiler_params=params(32),
        cost_estimate=cost(8 * rounds * rows * bnd * width, rounds * rows * bnd * 2),
        name="middle",
    )(
        local,
        bnd_tiles,
        wide,
        cotangent,
        w_self,
        w_neigh,
        bias.reshape(1, hidden),
        *incoming,
    )
    return results[0], results[1], results[2], results[3], results[4:]


def spread_kernel(scale, parts_ref, out_hbm, wide_ref, sem):
    total = parts_ref[0].astype(F32)
    for number in range(1, parts_ref.shape[0]):
        total = total + parts_ref[number].astype(F32)
    total = (total * scale).astype(wide_ref.dtype)
    for number in range(wide_ref.shape[0]):
        wide_ref[number] = total
    copy = pltpu.make_async_copy(wide_ref, out_hbm, sem)
    copy.start()
    copy.wait()


def sum_and_spread(parts, copies, dtype, scale):
    shape = (copies,) + parts.shape[1:]
    return pl.pallas_call(
        functools.partial(spread_kernel, scale),
        in_specs=[VMEM],
        out_specs=ANY,
        out_shape=pltpu.HBM(shape, dtype),
        scratch_shapes=[pltpu.VMEM(shape, dtype), DMA(())],
        compiler_params=params(16),
        name="sum_and_spread",
    )(parts)


def finish_kernel(adj_hbm, dagg_ref, gself_ref, index_ref, *refs):
    back_refs, (out_ref, adj_ref, base_ref, sems) = refs[:-4], refs[-4:]
    rows = adj_hbm.shape[0]
    spans = [pl.ds(start, BLOCK) for start in range(0, rows, BLOCK)]
    copies = [
        pltpu.make_async_copy(adj_hbm.at[span, :], adj_ref.at[span, :], sems.at[number])
        for number, span in enumerate(spans)
    ]
    for copy in copies:
        copy.start()
    base = gself_ref[...]
    for turn, back_ref in enumerate(back_refs):
        base = base + dot(one_hot(index_ref[turn], rows), back_ref[...])
    base_ref[...] = base
    turned = dagg_ref[...].T
    total = None
    for copy, span in zip(copies, spans):
        copy.wait()
        part = dot(turned[:, span.start : span.start + BLOCK], adj_ref[span, :])
        total = part if total is None else total + part
    out_ref[...] = (base_ref[...] + total.T).astype(out_ref.dtype)


def finish(local_adj, dagg, gself, index_lists, returned):
    rows, width = dagg.shape
    return pl.pallas_call(
        finish_kernel,
        in_specs=[ANY] + [VMEM] * (3 + len(returned)),
        out_shape=jax.ShapeDtypeStruct((rows, width), BF16),
        scratch_shapes=[
            pltpu.VMEM((rows, rows), BF16),
            pltpu.VMEM((rows, width), F32),
            DMA((rows // BLOCK,)),
        ],
        compiler_params=params(24),
        cost_estimate=cost(4 * rows * rows * width, rows * rows * 2),
        name="finish",
    )(in_hbm(local_adj), dagg, gself, index_lists, *returned)


def swapped(block, bit):
    count = math.prod(lax.axis_size(axis) for axis in AXES)
    return lax.ppermute(block, AXES, [(low, low ^ 1 << bit) for low in range(count)])


def after(value, *others):
    return lax.optimization_barrier((value, *others))[0]


def per_device(feats, local_adj, bnd_adj, send_index, w_self, w_neigh, bias, cotangent):
    chips = math.prod(lax.axis_size(axis) for axis in AXES[:-1])
    cores = lax.axis_size(AXES[-1])
    bits = chips.bit_length() - 1
    bnd_tiles = bnd_adj[0]
    rounds, _, picks = bnd_tiles.shape
    index_lists = send_index.reshape(rounds, 1, -1)
    rows, width = feats.shape

    def partner(turn):
        return bits - turn % bits

    outgoing, wide, near_adj = gather_rows(feats, index_lists, local_adj)
    incoming = [swapped(outgoing[turn], partner(turn)) for turn in ORDER]
    first, last = ORDER[:EARLY], ORDER[EARLY:]
    local = early_sum(near_adj, wide, bnd_tiles, first, incoming[:EARLY])
    output, dagg, gself, gw, back = middle(
        local, bnd_tiles, wide, cotangent, w_self, w_neigh, bias, last, incoming[EARLY:]
    )

    plane = math.prod(lax.axis_size(axis) for axis in PLANE)
    planes = chips * cores // plane
    pieces = gw.reshape(plane, -1, width)
    pieces = lax.all_to_all(pieces, PLANE, 0, 0, tiled=True)
    far = (2, 0, 4)
    near = (1, 3, 5)
    returned = {turn: swapped(back[turn], partner(turn)) for turn in far}
    pieces = sum_and_spread(pieces, planes, F32, 1.0)
    pieces = lax.all_to_all(pieces, AXES[:1], 0, 0, tiled=True)
    for turn in near:
        returned[turn] = swapped(after(back[turn], *[returned[other] for other in far]), partner(turn))
    scale = 1.0 / math.sqrt(rows * chips * cores)
    pieces = sum_and_spread(pieces, plane, BF16, scale)
    pieces = lax.all_to_all(pieces, PLANE, 0, 0, tiled=True)
    grad_feats = finish(
        local_adj, dagg, gself, index_lists, [returned[turn] for turn in range(rounds)]
    )
    sums = jnp.concatenate([*pieces.reshape(gw.shape)], axis=1).astype(F32)
    return output, grad_feats, sums[:width], sums[width:]


def solution(mesh):
    chips = mesh.shape["dom"] // SIDE**2
    shape = (chips, SIDE, SIDE, mesh.shape["grp"])
    mesh = Mesh(mesh.devices.reshape(shape), AXES)
    placed = (
        P(AXES, None),
        P(AXES, None),
        P(AXES, None, None, None),
        P(AXES, None, None),
        P(),
        P(),
        P(),
        P(AXES, None),
    )
    return jax.shard_map(
        per_device,
        mesh=mesh,
        in_specs=placed,
        out_specs=(P(AXES, None), P(AXES, None), P(), P()),
        check_vma=False,
    )
```

```python
import functools
import math

import jax
import jax.numpy as jnp
from jax import lax
from jax.experimental import pallas as pl
from jax.experimental.pallas import tpu as pltpu
from jax.sharding import Mesh
from jax.sharding import PartitionSpec as P

F32 = jnp.float32
BF16 = jnp.bfloat16
BLOCK = 384
ORDER = (2, 3, 1, 0, 5, 4)
EARLY = 3
SIDE = 4
AXES = ("z", "y", "x", "core")
PLANE = AXES[1:]


def dot(left, right, left_dim=1, right_dim=0):
    return lax.dot_general(
        left, right, (((left_dim,), (right_dim,)), ((), ())), preferred_element_type=F32
    )


def cost(flops, nbytes):
    return pl.CostEstimate(flops=int(flops), bytes_accessed=int(nbytes), transcendentals=0)


def params(mib):
    return pltpu.CompilerParams(vmem_limit_bytes=mib * 1024 * 1024)


def one_hot(index_row, count):
    places = lax.broadcasted_iota(jnp.int32, (count, index_row.shape[1]), 0)
    return (places == index_row).astype(F32).astype(BF16)


def in_hbm(array):
    return pltpu.with_memory_space_constraint(array, pltpu.HBM)


ANY = pl.BlockSpec(memory_space=pl.ANY)
VMEM = pl.BlockSpec(memory_space=pltpu.VMEM)
DMA = pltpu.SemaphoreType.DMA


def gather_kernel(rounds, feats_hbm, index_hbm, adj_hbm, *refs):
    out_refs, (wide_ref, adj_ref, index_ref, sems) = refs[:rounds], refs[rounds:]
    rows, width = feats_hbm.shape
    copies = [
        pltpu.make_async_copy(index_hbm, index_ref, sems.at[0]),
        pltpu.make_async_copy(feats_hbm, wide_ref.at[:, pl.ds(0, width)], sems.at[1]),
        pltpu.make_async_copy(adj_hbm, adj_ref, sems.at[2]),
    ]
    for copy in copies:
        copy.start()
    wide_ref[:, width:] = jnp.ones((rows, width), BF16)
    copies[0].wait()
    copies[1].wait()
    turned = wide_ref[:, :width].T
    for turn, out_ref in enumerate(out_refs):
        out_ref[...] = dot(turned, one_hot(index_ref[turn], rows)).T.astype(BF16)
    copies[2].wait()


def gather_rows(feats, index_lists, local_adj):
    rounds, _, picks = index_lists.shape
    rows, width = feats.shape
    results = pl.pallas_call(
        functools.partial(gather_kernel, rounds),
        in_specs=[ANY, ANY, ANY],
        out_specs=[VMEM] * (rounds + 2),
        out_shape=[jax.ShapeDtypeStruct((picks, width), BF16)] * rounds
        + [pltpu.VMEM((rows, 2 * width), BF16), pltpu.VMEM(local_adj.shape, BF16)],
        scratch_shapes=[pltpu.VMEM(index_lists.shape, jnp.int32), DMA((3,))],
        compiler_params=params(24),
        cost_estimate=cost(2 * rows * picks * width * rounds, rows * width * 2),
        name="gather_rows",
    )(in_hbm(feats), in_hbm(index_lists), in_hbm(local_adj))
    return results[:rounds], results[rounds], results[rounds + 1]


def widen(wide_ref, recv_refs):
    picks, width = recv_refs[0].shape
    for number, recv_ref in enumerate(recv_refs):
        span = slice(number * picks, (number + 1) * picks)
        wide_ref[span, :width] = recv_ref[...]
        wide_ref[span, width:] = jnp.ones((picks, width), BF16)


def tiles_of(bnd_ref, span, turns):
    return jnp.concatenate([bnd_ref[turn, span, :] for turn in turns], axis=1)


def early_kernel(turns, adj_ref, wide_ref, bnd_ref, *refs):
    recv_refs, (out_ref, recv_wide_ref) = refs[: len(turns)], refs[len(turns) :]
    widen(recv_wide_ref, recv_refs)
    for start in range(0, adj_ref.shape[0], BLOCK):
        span = slice(start, start + BLOCK)
        total = dot(adj_ref[span, :], wide_ref[...])
        out_ref[span, :] = total + dot(tiles_of(bnd_ref, span, turns), recv_wide_ref[...])


def early_sum(local_adj, wide, bnd_tiles, turns, incoming):
    rows, picks = local_adj.shape[0], bnd_tiles.shape[2]
    return pl.pallas_call(
        functools.partial(early_kernel, turns),
        out_shape=jax.ShapeDtypeStruct(wide.shape, F32),
        scratch_shapes=[pltpu.VMEM((len(turns) * picks, wide.shape[1]), BF16)],
        compiler_params=params(16),
        cost_estimate=cost(2 * rows * rows * wide.shape[1], rows * rows * 2),
        name="early_sum",
    )(local_adj, wide, bnd_tiles, *incoming)


def middle_kernel(turns, *refs):
    local_ref, bnd_ref, feats_ref, cot_ref, self_ref, neigh_ref, bias_ref = refs[:7]
    rounds = bnd_ref.shape[0]
    recv_refs, refs = refs[7 : 7 + len(turns)], refs[7 + len(turns) :]
    out_hbm, dagg_ref, gself_ref, gw_hbm = refs[:4]
    back_refs = refs[4 : 4 + rounds]
    wide_ref, both_ref, dpre_ref, inverse_ref, out_ref, gw_ref, sems = refs[4 + rounds :]
    rows, width = dagg_ref.shape
    spans = [slice(start, start + BLOCK) for start in range(0, rows, BLOCK)]

    widen(wide_ref, recv_refs)
    both_ref[:, :width] = feats_ref[:, :width]
    for span in spans:
        total = local_ref[span, :] + dot(tiles_of(bnd_ref, span, turns), wide_ref[...])
        inverse = 1.0 / (1.0 + total[:, width:])
        inverse_ref[span, :] = inverse
        both_ref[span, width:] = (total[:, :width] * inverse).astype(BF16)

    weights = jnp.concatenate([self_ref[...], neigh_ref[...]], axis=0)
    for span in spans:
        pre = dot(both_ref[span, :], weights) + bias_ref[...]
        sig = 0.5 + 0.5 * jnp.tanh(0.5 * pre)
        out = pre * sig
        out_ref[span, :] = out.astype(BF16)
        slope = sig * (1.0 + (pre - out))
        dpre_ref[span, :] = (cot_ref[span, :].astype(F32) * slope).astype(BF16)

    gw = dot(both_ref[...], dpre_ref[...], 0, 0).astype(BF16)
    for half in range(gw.shape[1] // width):
        gw_ref[half] = gw[:, half * width : (half + 1) * width]
    gw_copy = pltpu.make_async_copy(gw_ref, gw_hbm, sems.at[0])
    gw_copy.start()
    out_copy = pltpu.make_async_copy(out_ref, out_hbm, sems.at[1])
    out_copy.start()

    for span in spans:
        grads = dot(dpre_ref[span, :], weights, 1, 1)
        gself_ref[span, :] = grads[:, :width]
        dagg_ref[span, :] = (grads[:, width:] * inverse_ref[span, :]).astype(BF16)

    turned = dagg_ref[...].T
    for turn in range(rounds):
        back_refs[turn][...] = dot(turned, bnd_ref[turn]).T.astype(BF16)
    gw_copy.wait()
    out_copy.wait()


def middle(local, bnd_tiles, wide, cotangent, w_self, w_neigh, bias, turns, incoming):
    rounds, rows, bnd = bnd_tiles.shape
    width, hidden = w_self.shape
    results = pl.pallas_call(
        functools.partial(middle_kernel, turns),
        in_specs=[VMEM] * (7 + len(turns)),
        out_specs=[ANY, VMEM, VMEM, ANY] + [VMEM] * rounds,
        out_shape=[
            pltpu.HBM((rows, hidden), BF16),
            jax.ShapeDtypeStruct((rows, width), BF16),
            jax.ShapeDtypeStruct((rows, width), F32),
            pltpu.HBM((hidden // width, 2 * width, width), BF16),
        ]
        + [jax.ShapeDtypeStruct((bnd, width), BF16)] * rounds,
        scratch_shapes=[
            pltpu.VMEM((len(turns) * bnd, 2 * width), BF16),
            pltpu.VMEM((rows, 2 * width), BF16),
            pltpu.VMEM((rows, hidden), BF16),
            pltpu.VMEM((rows, width), F32),
            pltpu.VMEM((rows, hidden), BF16),
            pltpu.VMEM((hidden // width, 2 * width, width), BF16),
            DMA((2,)),
        ],
        compiler_params=params(32),
        cost_estimate=cost(8 * rounds * rows * bnd * width, rounds * rows * bnd * 2),
        name="middle",
    )(
        local,
        bnd_tiles,
        wide,
        cotangent,
        w_self,
        w_neigh,
        bias.reshape(1, hidden),
        *incoming,
    )
    return results[0], results[1], results[2], results[3], results[4:]


def spread_kernel(scale, parts_ref, out_hbm, wide_ref, sem):
    total = parts_ref[0].astype(F32)
    for number in range(1, parts_ref.shape[0]):
        total = total + parts_ref[number].astype(F32)
    total = (total * scale).astype(wide_ref.dtype)
    for number in range(wide_ref.shape[0]):
        wide_ref[number] = total
    copy = pltpu.make_async_copy(wide_ref, out_hbm, sem)
    copy.start()
    copy.wait()


def sum_and_spread(parts, copies, dtype, scale):
    shape = (copies,) + parts.shape[1:]
    return pl.pallas_call(
        functools.partial(spread_kernel, scale),
        in_specs=[VMEM],
        out_specs=ANY,
        out_shape=pltpu.HBM(shape, dtype),
        scratch_shapes=[pltpu.VMEM(shape, dtype), DMA(())],
        compiler_params=params(16),
        name="sum_and_spread",
    )(parts)


def finish_kernel(adj_hbm, dagg_ref, gself_ref, index_ref, *refs):
    back_refs, (out_ref, adj_ref, base_ref, sems) = refs[:-4], refs[-4:]
    rows = adj_hbm.shape[0]
    spans = [pl.ds(start, BLOCK) for start in range(0, rows, BLOCK)]
    copies = [
        pltpu.make_async_copy(adj_hbm.at[span, :], adj_ref.at[span, :], sems.at[number])
        for number, span in enumerate(spans)
    ]
    for copy in copies:
        copy.start()
    picked = jnp.concatenate([index_ref[turn] for turn in range(len(back_refs))], axis=1)
    backs = jnp.concatenate([back_ref[...] for back_ref in back_refs], axis=0)
    for start in range(0, rows, BLOCK):
        span = slice(start, start + BLOCK)
        base_ref[span, :] = gself_ref[span, :] + dot(one_hot(picked - start, BLOCK), backs)
    turned = dagg_ref[...].T
    for copy in copies:
        copy.wait()
    out_ref[...] = (base_ref[...] + dot(turned, adj_ref[...]).T).astype(out_ref.dtype)


def finish(local_adj, dagg, gself, index_lists, returned):
    rows, width = dagg.shape
    return pl.pallas_call(
        finish_kernel,
        in_specs=[ANY] + [VMEM] * (3 + len(returned)),
        out_shape=jax.ShapeDtypeStruct((rows, width), BF16),
        scratch_shapes=[
            pltpu.VMEM((rows, rows), BF16),
            pltpu.VMEM((rows, width), F32),
            DMA((rows // BLOCK,)),
        ],
        compiler_params=params(24),
        cost_estimate=cost(4 * rows * rows * width, rows * rows * 2),
        name="finish",
    )(in_hbm(local_adj), dagg, gself, index_lists, *returned)


def swapped(block, bit):
    count = math.prod(lax.axis_size(axis) for axis in AXES)
    return lax.ppermute(block, AXES, [(low, low ^ 1 << bit) for low in range(count)])


def after(value, *others):
    return lax.optimization_barrier((value, *others))[0]


def per_device(feats, local_adj, bnd_adj, send_index, w_self, w_neigh, bias, cotangent):
    chips = math.prod(lax.axis_size(axis) for axis in AXES[:-1])
    cores = lax.axis_size(AXES[-1])
    bits = chips.bit_length() - 1
    bnd_tiles = bnd_adj[0]
    rounds, _, picks = bnd_tiles.shape
    index_lists = send_index.reshape(rounds, 1, -1)
    rows, width = feats.shape

    def partner(turn):
        return bits - turn % bits

    outgoing, wide, near_adj = gather_rows(feats, index_lists, local_adj)
    incoming = [swapped(outgoing[turn], partner(turn)) for turn in ORDER]
    first, last = ORDER[:EARLY], ORDER[EARLY:]
    local = early_sum(near_adj, wide, bnd_tiles, first, incoming[:EARLY])
    output, dagg, gself, gw, back = middle(
        local, bnd_tiles, wide, cotangent, w_self, w_neigh, bias, last, incoming[EARLY:]
    )

    plane = math.prod(lax.axis_size(axis) for axis in PLANE)
    planes = chips * cores // plane
    pieces = gw.reshape(plane, -1, width)
    pieces = lax.all_to_all(pieces, PLANE, 0, 0, tiled=True)
    far = (2, 0, 4)
    near = (1, 3, 5)
    returned = {turn: swapped(back[turn], partner(turn)) for turn in far}
    pieces = sum_and_spread(pieces, planes, F32, 1.0)
    pieces = lax.all_to_all(pieces, AXES[:1], 0, 0, tiled=True)
    for turn in near:
        returned[turn] = swapped(after(back[turn], *[returned[other] for other in far]), partner(turn))
    scale = 1.0 / math.sqrt(rows * chips * cores)
    pieces = sum_and_spread(pieces, plane, BF16, scale)
    pieces = lax.all_to_all(pieces, PLANE, 0, 0, tiled=True)
    grad_feats = finish(
        local_adj, dagg, gself, index_lists, [returned[turn] for turn in range(rounds)]
    )
    sums = jnp.concatenate([*pieces.reshape(gw.shape)], axis=1).astype(F32)
    return output, grad_feats, sums[:width], sums[width:]


def solution(mesh):
    chips = mesh.shape["dom"] // SIDE**2
    shape = (chips, SIDE, SIDE, mesh.shape["grp"])
    mesh = Mesh(mesh.devices.reshape(shape), AXES)
    placed = (
        P(AXES, None),
        P(AXES, None),
        P(AXES, None, None, None),
        P(AXES, None, None),
        P(),
        P(),
        P(),
        P(AXES, None),
    )
    return jax.shard_map(
        per_device,
        mesh=mesh,
        in_specs=placed,
        out_specs=(P(AXES, None), P(AXES, None), P(), P()),
        check_vma=False,
    )
```
